32 devices in a mesh: dp: 16 (over z, y, core), seq: 2 (over x).
Axes of the slice: x: 2, y: 2, z: 4, core: 2. Of those that a mesh axis runs over, the one named last changes fastest.
Arguments:
- queries: bfloat16 [4096, 4096], P(('dp', 'seq')), may hold values from -180 to 180, as said below
- keys: bfloat16 [4096, 512], P(('dp', 'seq')), may hold values from -6 to 6, as said below
- values: bfloat16 [4096, 512], P(('dp', 'seq')), may hold values from -6 to 6
- lengths: int32 [16, 16], P('dp'), may hold values from 1 to 128, 256 in all within a row
- out_grad: bfloat16 [4096, 4096], P(('dp', 'seq')), may hold values from -6 to 6
Outputs:
- attended: bfloat16 [4096, 4096], P(('dp', 'seq'))
- query_grad: bfloat16 [4096, 4096], P(('dp', 'seq'))
- key_grad: bfloat16 [4096, 512], P(('dp', 'seq'))
- value_grad: bfloat16 [4096, 512], P(('dp', 'seq'))
The draws below stay inside these ranges and needn't reach their ends.
Inputs may be any that keep to these rules, and one draw needn't show every extreme that they name: `queries`: queries stay within this range. `keys`: keys stay within this range.
All inputs are finite; a program needn't handle non-finite values.
Results may differ from the reference program's by a relative error of at most 0.0095.
Values may be sent and summed in bfloat16 or wider, within the bound.
A program may use at most 64 MiB of HBM per device.

```python
import math
import jax
import jax.numpy as jnp
import numpy as np
from jax import lax

H = 32
KVH = 4
HD = 128
GROUP = 8
SEGS = 16
LEN = 256
MOST = 128
BATCH_TOK = 4096
N_DP = 16
N_SEQ = 2


def draw_pair(key):
    base_q = jnp.clip(jax.random.normal(jax.random.fold_in(key, 11), (BATCH_TOK, KVH, GROUP, HD), jnp.float32), -6.0, 6.0)
    base_k = jnp.clip(jax.random.normal(jax.random.fold_in(key, 12), (BATCH_TOK, KVH, HD), jnp.float32), -6.0, 6.0)
    return (base_q.reshape(BATCH_TOK, H * HD), base_k.reshape(BATCH_TOK, KVH * HD))


def draw_queries(key, part):
    return draw_pair(key)[0].astype(jnp.bfloat16)


def draw_keys(key, part):
    return draw_pair(key)[1].astype(jnp.bfloat16)


def block_levels(key, extent, pieces, low, top_value):
    factor_of, own = 1.0, jax.random.fold_in(key, 6)
    for position, parts in pieces:
        heights = jnp.exp(jax.random.uniform(jax.random.fold_in(own, position), (parts,), jnp.float32, low / len(pieces), top_value / len(pieces)))
        factor_of = factor_of * jnp.repeat(heights, extent[position] // parts).reshape([-1 if axis == position else 1 for axis in range(len(extent))])
    return factor_of


def profile(count, total, reach, lean):
    weights = [(1 << 20) // math.isqrt(grade ** lean) + 1 for grade in range(2, count + 1)]
    spare, given = total - reach - (count - 1), [1] * (count - 1)
    while spare > 0:
        free = [i for i in range(count - 1) if given[i] < reach]
        pool, budget = sum([weights[i] for i in free]), spare
        for i in free:
            more = min(reach - given[i], max(1, budget * weights[i] // pool), spare)
            given[i] = given[i] + more
            spare = spare - more
    return np.array([reach] + given)


def uneven(stream_key, count, total, reach, slope):
    if count == 2:
        one = jax.random.randint(stream_key, (), max(1, total - reach), min(reach, total - 1) + 1)
        return jnp.stack([one, total - one])
    tallies = jnp.asarray(profile(count, total, reach, slope), jnp.int32)
    twos = (count - 1) // 2
    donor, sink = tallies[1:1 + 2 * twos:2], tallies[2:2 + 2 * twos:2]
    room = jnp.minimum(donor - 1, reach - sink)
    passed = jax.random.randint(jax.random.fold_in(stream_key, 1), (twos,), 0, 1 << 20) % (room + 1)
    tallies = tallies.at[1:1 + 2 * twos:2].set(donor - passed).at[2:2 + 2 * twos:2].set(sink + passed)
    return tallies[jax.random.permutation(jax.random.fold_in(stream_key, 2), count)]


def centred(own_key, dims, deviation, bound, cuts=(), held_as=jnp.bfloat16):
    result = jax.random.normal(own_key, dims, jnp.float32) * deviation
    if len(cuts) > 0:
        result = block_levels(own_key, dims, cuts, -0.22, 0.18) * result
    return jnp.clip(result, min=-bound, max=bound).astype(held_as)


def setup_inputs(seed: int = 0) -> dict:
    seeds = jax.random.split(jax.random.key(seed), 6)
    queries = draw_queries(jax.random.fold_in(seeds[5], 71), 0)
    keys = draw_keys(jax.random.fold_in(seeds[5], 71), 0)
    values = centred(seeds[2], (BATCH_TOK, KVH * HD), 1.0, 6.0, ((0, 32),))
    lengths = jax.vmap(lambda own: uneven(own, SEGS, LEN, MOST, 2))(jax.random.split(seeds[3], N_DP)).reshape((N_DP, SEGS)).astype(jnp.int32)
    out_grad = centred(seeds[4], (BATCH_TOK, H * HD), 1.0, 6.0, ((0, 32),))
    return dict(queries=queries, keys=keys, values=values, lengths=lengths, out_grad=out_grad)


def doc_of(pos, ends):
    return jnp.sum((pos[:, None] >= ends[None, :]).astype(jnp.int32), axis=1)


def one_sequence(args):
    queries, keys, values, lens, out_grad = args
    scale = HD ** -0.5
    qh = queries.astype(jnp.float32).reshape(LEN, KVH, GROUP, HD)
    kh = keys.astype(jnp.float32).reshape(LEN, KVH, HD)
    vh = values.astype(jnp.float32).reshape(LEN, KVH, HD)
    gh = out_grad.astype(jnp.float32).reshape(LEN, KVH, GROUP, HD)
    ends = jnp.cumsum(lens).astype(jnp.int32)
    pos = jnp.arange(LEN, dtype=jnp.int32)
    docs = doc_of(pos, ends)
    visible = (docs[:, None] == docs[None, :]) & (pos[None, :] <= pos[:, None])
    scores = jnp.einsum('tkgd,skd->kgts', qh, kh) * scale
    scores = jnp.where(visible, scores, -1e30)
    top = jnp.max(scores, axis=-1)
    expo = jnp.where(visible, jnp.exp(scores - top[..., None]), 0.0)
    lsum = jnp.sum(expo, axis=-1)
    weights = lax.optimization_barrier(expo.astype(jnp.bfloat16)).astype(jnp.float32)
    heads_out = jnp.einsum('kgts,skd->kgtd', weights, vh) / lsum[..., None]
    attended = heads_out.transpose(2, 0, 1, 3).reshape(LEN, H * HD).astype(jnp.bfloat16)
    rowdot = jnp.sum(gh * attended.astype(jnp.float32).reshape(LEN, KVH, GROUP, HD), axis=-1).transpose(1, 2, 0)
    probs = expo / lsum[..., None]
    probs_b = lax.optimization_barrier(probs.astype(jnp.bfloat16)).astype(jnp.float32)
    dprobs = jnp.einsum('tkgd,skd->kgts', gh, vh)
    dscores = lax.optimization_barrier((probs * (dprobs - rowdot[..., None])).astype(jnp.bfloat16)).astype(jnp.float32)
    query_grad = (jnp.einsum('kgts,skd->kgtd', dscores, kh) * scale).transpose(2, 0, 1, 3).reshape(LEN, H * HD).astype(jnp.bfloat16)
    runs = LEN // N_SEQ
    ds_runs = dscores.reshape(KVH, GROUP, N_SEQ, runs, LEN)
    pb_runs = probs_b.reshape(KVH, GROUP, N_SEQ, runs, LEN)
    q_runs = qh.reshape(N_SEQ, runs, KVH, GROUP, HD)
    g_runs = gh.reshape(N_SEQ, runs, KVH, GROUP, HD)
    key_parts = (jnp.einsum('kgjts,jtkgd->jskd', ds_runs, q_runs) * scale).astype(jnp.bfloat16).astype(jnp.float32)
    value_parts = jnp.einsum('kgjts,jtkgd->jskd', pb_runs, g_runs).astype(jnp.bfloat16).astype(jnp.float32)
    key_grad = jnp.sum(key_parts, axis=0).reshape(LEN, KVH * HD).astype(jnp.bfloat16)
    value_grad = jnp.sum(value_parts, axis=0).reshape(LEN, KVH * HD).astype(jnp.bfloat16)
    return attended, query_grad, key_grad, value_grad


def reference(queries, keys, values, lengths, out_grad):
    split = (queries.reshape(N_DP, LEN, H * HD), keys.reshape(N_DP, LEN, KVH * HD),
             values.reshape(N_DP, LEN, KVH * HD), lengths, out_grad.reshape(N_DP, LEN, H * HD))
    attended, query_grad, key_grad, value_grad = lax.map(one_sequence, split)
    return (attended.reshape(BATCH_TOK, H * HD), query_grad.reshape(BATCH_TOK, H * HD),
            key_grad.reshape(BATCH_TOK, KVH * HD), value_grad.reshape(BATCH_TOK, KVH * HD))
```

```python
import functools

import jax
import jax.numpy as jnp
from jax import lax
from jax.experimental import pallas as pl
from jax.experimental.pallas import tpu as pltpu
from jax.sharding import PartitionSpec as P

H = 32
KVH = 4
HD = 128
GROUP = 8
SCALE = HD ** (-0.5)
EXP2_SCALE = SCALE * 1.4426950408889634
NT = (((1,), (1,)), ((), ()))
NN = (((1,), (0,)), ((), ()))


def dot(a, b, dims):
    return lax.dot_general(a, b, dims, preferred_element_type=jnp.float32)


def lanes(index, width):
    return pl.ds(pl.multiple_of(index * width, 128), width)


def kernel(
    n, rows, segs,
    lens, q_in, k_in, v_in, g_in,
    att_out, dq_out, dk_out, dv_out,
    q, g, qt, gt, att, dq, bias,
    kv, part, got, own,
    load_sem, own_sem, store_sem, final_sem,
    kv_send, kv_recv, part_send, part_recv,
):
    me = lax.axis_index("seq")
    barrier = pltpu.get_barrier_semaphore()
    for step in range(1, n):
        pl.semaphore_signal(
            barrier, inc=1, device_id={"seq": lax.rem(me + step, n)},
            device_id_type=pl.DeviceIdType.MESH,
        )

    wide = GROUP * HD
    sources = (k_in, v_in)

    def load(which, k):
        return pltpu.make_async_copy(
            (q_in, g_in)[which].at[:, lanes(k, wide)],
            (q, g)[which].at[:, lanes(k, wide)],
            load_sem.at[which, k],
        )

    def store(which, k):
        return pltpu.make_async_copy(
            (att, dq)[which].at[:, lanes(k, wide)],
            (att_out, dq_out)[which].at[:, lanes(k, wide)],
            store_sem.at[which, k],
        )

    def send_kv(which, k, src, dst):
        return pltpu.make_async_remote_copy(
            src_ref=sources[which].at[:, lanes(k, HD)],
            dst_ref=kv.at[which, pl.ds(src * rows, rows), lanes(k, HD)],
            send_sem=kv_send.at[which, k, dst],
            recv_sem=kv_recv.at[which, k, src],
            device_id={"seq": dst},
            device_id_type=pl.DeviceIdType.MESH,
        )

    def send_part(which, k, src, dst):
        return pltpu.make_async_remote_copy(
            src_ref=part.at[which, pl.ds(dst * rows, rows), lanes(k, HD)],
            dst_ref=got.at[which, pl.ds(src * rows, rows), lanes(k, HD)],
            send_sem=part_send.at[which, k, dst],
            recv_sem=part_recv.at[which, k, src],
            device_id={"seq": dst},
            device_id_type=pl.DeviceIdType.MESH,
        )

    def on_device(m):
        length = (m + 1) * rows
        heads = GROUP
        while heads > 1 and heads * rows * length > 1 << 18:
            heads //= 2

        own_copies = [
            pltpu.make_async_copy(
                sources[which], kv.at[which, pl.ds(m * rows, rows), :], own_sem.at[which]
            )
            for which in range(2)
        ]
        for which in range(2):
            own_copies[which].start()
        for k in range(KVH):
            load(0, k).start()
            load(1, k).start()
        pl.semaphore_wait(barrier, n - 1)
        for k in range(KVH):
            for dst in range(m + 1, n):
                send_kv(0, k, m, dst).start()
                send_kv(1, k, m, dst).start()

        pos = lax.broadcasted_iota(jnp.int32, (rows, 128), 0) + m * rows
        first = jnp.zeros((rows, 128), jnp.int32)
        end = jnp.int32(0)
        for seg in range(segs):
            end = end + lens[0, seg]
            first = jnp.maximum(first, jnp.where(pos >= end, end, 0))
        for c in range(length // 128):
            col = lax.broadcasted_iota(jnp.int32, (rows, 128), 1) + c * 128
            seen = (col >= first) & (col <= pos)
            bias[:, c * 128:(c + 1) * 128] = jnp.where(seen, 0.0, -1e30)

        @pl.loop(0, KVH)
        def _(k):
            load(0, k).wait()
            load(1, k).wait()
            for h in range(GROUP):
                head = k * GROUP + h
                qt[:, lanes(head, rows)] = q[:, lanes(head, HD)].T
                gt[:, lanes(head, rows)] = g[:, lanes(head, HD)].T

        for which in range(2):
            own_copies[which].wait()

        @pl.loop(0, KVH)
        def _(k):
            for src in range(m):
                send_kv(0, k, src, src).wait_recv()
                send_kv(1, k, src, src).wait_recv()
            key = kv[0, 0:length, lanes(k, HD)]
            value = kv[1, 0:length, lanes(k, HD)]
            dkt = jnp.zeros((HD, length), jnp.float32)
            dvt = jnp.zeros((HD, length), jnp.float32)
            for base in range(0, GROUP, heads):
                ids = [k * GROUP + base + h for h in range(heads)]
                qs = jnp.concatenate([q[:, lanes(i, HD)] for i in ids], axis=0)
                gs = jnp.concatenate([g[:, lanes(i, HD)] for i in ids], axis=0)
                raw = dot(qs, key, NT).reshape(heads, rows, length)
                raw = (raw + bias[:, 0:length][None]).reshape(heads * rows, length)
                top = jnp.max(raw, axis=-1, keepdims=True)
                expo = jnp.exp2((raw - top) * EXP2_SCALE)
                inv = 1.0 / jnp.sum(expo, axis=-1, keepdims=True)
                out = (dot(expo.astype(jnp.bfloat16), value, NN) * inv).astype(jnp.bfloat16)
                rowdot = jnp.sum(
                    gs.astype(jnp.float32) * out.astype(jnp.float32), axis=-1, keepdims=True
                )
                probs = expo * inv
                dscores = (probs * (dot(gs, value, NT) - rowdot)).astype(jnp.bfloat16)
                grad = (dot(dscores, key, NN) * SCALE).astype(jnp.bfloat16)
                for h in range(heads):
                    att[:, lanes(ids[h], HD)] = out[h * rows:(h + 1) * rows]
                    dq[:, lanes(ids[h], HD)] = grad[h * rows:(h + 1) * rows]
                span = pl.ds(pl.multiple_of(ids[0] * rows, 128), heads * rows)
                dkt += dot(qt[:, span], dscores, NN)
                dvt += dot(gt[:, span], probs.astype(jnp.bfloat16), NN)
            part[0, 0:length, lanes(k, HD)] = (dkt.T * SCALE).astype(jnp.bfloat16)
            part[1, 0:length, lanes(k, HD)] = dvt.T.astype(jnp.bfloat16)
            for dst in range(m):
                send_part(0, k, m, dst).start()
                send_part(1, k, m, dst).start()
            store(0, k).start()
            store(1, k).start()

        mine = pl.ds(m * rows, rows)
        finals = []
        for which in range(2):
            final = part.at[which, mine, :]
            if m < n - 1:
                final = own.at[which]
            finals.append(
                pltpu.make_async_copy(final, (dk_out, dv_out)[which], final_sem.at[which])
            )
        if m < n - 1:
            for k in range(KVH):
                for which in range(2):
                    total = part[which, mine, lanes(k, HD)].astype(jnp.float32)
                    for src in range(m + 1, n):
                        send_part(which, k, src, src).wait_recv()
                        total += got[which, pl.ds(src * rows, rows), lanes(k, HD)].astype(
                            jnp.float32
                        )
                    own[which, :, lanes(k, HD)] = total.astype(jnp.bfloat16)
        for which in range(2):
            finals[which].start()
        for k in range(KVH):
            for which in range(2):
                store(which, k).wait()
                for dst in range(m + 1, n):
                    send_kv(which, k, m, dst).wait_send()
                for dst in range(m):
                    send_part(which, k, m, dst).wait_send()
        for which in range(2):
            finals[which].wait()

    for m in range(n):
        pl.when(me == m)(functools.partial(on_device, m))


def shards(n, queries, keys, values, lengths, out_grad):
    rows = queries.shape[0]
    segs = lengths.shape[1]
    total = n * rows
    bf16 = jnp.bfloat16
    dma = pltpu.SemaphoreType.DMA
    wide = jax.ShapeDtypeStruct(queries.shape, bf16)
    thin = jax.ShapeDtypeStruct(keys.shape, bf16)
    anywhere = pl.BlockSpec(memory_space=pl.ANY)
    return pl.pallas_call(
        functools.partial(kernel, n, rows, segs),
        out_shape=(wide, wide, thin, thin),
        in_specs=[pl.BlockSpec(memory_space=pltpu.SMEM)] + [anywhere] * 4,
        out_specs=(anywhere,) * 4,
        scratch_shapes=[
            pltpu.VMEM((rows, H * HD), bf16),
            pltpu.VMEM((rows, H * HD), bf16),
            pltpu.VMEM((HD, H * rows), bf16),
            pltpu.VMEM((HD, H * rows), bf16),
            pltpu.VMEM((rows, H * HD), bf16),
            pltpu.VMEM((rows, H * HD), bf16),
            pltpu.VMEM((rows, total), jnp.float32),
            pltpu.VMEM((2, total, KVH * HD), bf16),
            pltpu.VMEM((2, total, KVH * HD), bf16),
            pltpu.VMEM((2, total, KVH * HD), bf16),
            pltpu.VMEM((2, rows, KVH * HD), bf16),
            dma((2, KVH)),
            dma((2,)),
            dma((2, KVH)),
            dma((2,)),
            dma((2, KVH, n)),
            dma((2, KVH, n)),
            dma((2, KVH, n)),
            dma((2, KVH, n)),
        ],
        compiler_params=pltpu.CompilerParams(
            collective_id=0, has_side_effects=True, vmem_limit_bytes=48 * 1024 * 1024
        ),
    )(lengths, queries, keys, values, out_grad)


def solution(mesh):
    rows = P(("dp", "seq"), None)
    return jax.shard_map(
        functools.partial(shards, mesh.shape["seq"]),
        mesh=mesh,
        in_specs=(rows, rows, rows, P("dp", None), rows),
        out_specs=(rows,) * 4,
        check_vma=False,
    )
```

```python
import functools

import jax
import jax.numpy as jnp
from jax import lax
from jax.experimental import pallas as pl
from jax.experimental.pallas import tpu as pltpu
from jax.sharding import PartitionSpec as P

H = 32
KVH = 4
HD = 128
GROUP = 8
SCALE = HD ** (-0.5)
EXP2_SCALE = SCALE * 1.4426950408889634
NT = (((1,), (1,)), ((), ()))
NN = (((1,), (0,)), ((), ()))


def dot(a, b, dims):
    return lax.dot_general(a, b, dims, preferred_element_type=jnp.float32)


def lanes(index, width):
    return pl.ds(pl.multiple_of(index * width, 128), width)


def kernel(
    n, rows, segs,
    lens_in, q_in, k_in, v_in, g_in,
    att_out, dq_out, dk_out, dv_out,
    lens, q, g, qt, gt, att, dq, bias,
    kv, part, got, own,
    lens_sem, load_sem, own_sem, store_sem, final_sem,
    kv_send, kv_recv, part_send, part_recv,
):
    me = lax.axis_index("seq")
    lens_copy = pltpu.make_async_copy(lens_in, lens, lens_sem)
    lens_copy.start()
    barrier = pltpu.get_barrier_semaphore()
    for step in range(1, n):
        pl.semaphore_signal(
            barrier, inc=1, device_id={"seq": lax.rem(me + step, n)},
            device_id_type=pl.DeviceIdType.MESH,
        )

    wide = GROUP * HD
    sources = (k_in, v_in)

    def load(which, k):
        return pltpu.make_async_copy(
            (q_in, g_in)[which].at[:, lanes(k, wide)],
            (q, g)[which].at[:, lanes(k, wide)],
            load_sem.at[which, k],
        )

    def store(which, k):
        return pltpu.make_async_copy(
            (att, dq)[which].at[:, lanes(k, wide)],
            (att_out, dq_out)[which].at[:, lanes(k, wide)],
            store_sem.at[which, k],
        )

    def send_kv(which, k, src, dst):
        return pltpu.make_async_remote_copy(
            src_ref=sources[which].at[:, lanes(k, HD)],
            dst_ref=kv.at[which, pl.ds(src * rows, rows), lanes(k, HD)],
            send_sem=kv_send.at[which, k, dst],
            recv_sem=kv_recv.at[which, k, src],
            device_id={"seq": dst},
            device_id_type=pl.DeviceIdType.MESH,
        )

    def send_part(which, k, src, dst):
        return pltpu.make_async_remote_copy(
            src_ref=part.at[which, pl.ds(dst * rows, rows), lanes(k, HD)],
            dst_ref=got.at[which, pl.ds(src * rows, rows), lanes(k, HD)],
            send_sem=part_send.at[which, k, dst],
            recv_sem=part_recv.at[which, k, src],
            device_id={"seq": dst},
            device_id_type=pl.DeviceIdType.MESH,
        )

    def on_device(m):
        length = (m + 1) * rows
        heads = GROUP
        while heads > 1 and heads * rows * length > 1 << 18:
            heads //= 2

        own_copies = [
            pltpu.make_async_copy(
                sources[which], kv.at[which, pl.ds(m * rows, rows), :], own_sem.at[which]
            )
            for which in range(2)
        ]
        for which in range(2):
            own_copies[which].start()
        for k in range(KVH):
            load(0, k).start()
            load(1, k).start()
        pl.semaphore_wait(barrier, n - 1)
        for k in range(KVH):
            for dst in range(m + 1, n):
                send_kv(0, k, m, dst).start()
                send_kv(1, k, m, dst).start()

        lens_copy.wait()
        pos = lax.broadcasted_iota(jnp.int32, (rows, 128), 0) + m * rows
        first = jnp.zeros((rows, 128), jnp.int32)
        end = jnp.int32(0)
        for seg in range(segs):
            end = end + lens[0, seg]
            first = jnp.maximum(first, jnp.where(pos >= end, end, 0))
        for c in range(length // 128):
            col = lax.broadcasted_iota(jnp.int32, (rows, 128), 1) + c * 128
            seen = (col >= first) & (col <= pos)
            bias[:, c * 128:(c + 1) * 128] = jnp.where(seen, 0.0, -1e30)

        @pl.loop(0, KVH)
        def _(k):
            load(0, k).wait()
            load(1, k).wait()
            for h in range(GROUP):
                head = k * GROUP + h
                qt[:, lanes(head, rows)] = q[:, lanes(head, HD)].T
                gt[:, lanes(head, rows)] = g[:, lanes(head, HD)].T

        for which in range(2):
            own_copies[which].wait()

        @pl.loop(0, KVH)
        def _(k):
            for src in range(m):
                send_kv(0, k, src, src).wait_recv()
                send_kv(1, k, src, src).wait_recv()
            key = kv[0, 0:length, lanes(k, HD)]
            value = kv[1, 0:length, lanes(k, HD)]
            dkt = jnp.zeros((HD, length), jnp.float32)
            dvt = jnp.zeros((HD, length), jnp.float32)
            for base in range(0, GROUP, heads):
                ids = [k * GROUP + base + h for h in range(heads)]
                qs = jnp.concatenate([q[:, lanes(i, HD)] for i in ids], axis=0)
                gs = jnp.concatenate([g[:, lanes(i, HD)] for i in ids], axis=0)
                raw = dot(qs, key, NT).reshape(heads, rows, length)
                raw = (raw + bias[:, 0:length][None]).reshape(heads * rows, length)
                top = jnp.max(raw, axis=-1, keepdims=True)
                expo = jnp.exp2((raw - top) * EXP2_SCALE)
                inv = 1.0 / jnp.sum(expo, axis=-1, keepdims=True)
                out = (dot(expo.astype(jnp.bfloat16), value, NN) * inv).astype(jnp.bfloat16)
                rowdot = jnp.sum(
                    gs.astype(jnp.float32) * out.astype(jnp.float32), axis=-1, keepdims=True
                )
                probs = expo * inv
                dscores = (probs * (dot(gs, value, NT) - rowdot)).astype(jnp.bfloat16)
                grad = (dot(dscores, key, NN) * SCALE).astype(jnp.bfloat16)
                for h in range(heads):
                    att[:, lanes(ids[h], HD)] = out[h * rows:(h + 1) * rows]
                    dq[:, lanes(ids[h], HD)] = grad[h * rows:(h + 1) * rows]
                span = pl.ds(pl.multiple_of(ids[0] * rows, 128), heads * rows)
                dkt += dot(qt[:, span], dscores, NN)
                dvt += dot(gt[:, span], probs.astype(jnp.bfloat16), NN)
            part[0, 0:length, lanes(k, HD)] = (dkt.T * SCALE).astype(jnp.bfloat16)
            part[1, 0:length, lanes(k, HD)] = dvt.T.astype(jnp.bfloat16)
            for dst in range(m):
                send_part(0, k, m, dst).start()
                send_part(1, k, m, dst).start()
            store(0, k).start()
            store(1, k).start()

        mine = pl.ds(m * rows, rows)
        finals = []
        for which in range(2):
            final = part.at[which, mine, :]
            if m < n - 1:
                final = own.at[which]
            finals.append(
                pltpu.make_async_copy(final, (dk_out, dv_out)[which], final_sem.at[which])
            )
        if m < n - 1:
            for k in range(KVH):
                for which in range(2):
                    total = part[which, mine, lanes(k, HD)].astype(jnp.float32)
                    for src in range(m + 1, n):
                        send_part(which, k, src, src).wait_recv()
                        total += got[which, pl.ds(src * rows, rows), lanes(k, HD)].astype(
                            jnp.float32
                        )
                    own[which, :, lanes(k, HD)] = total.astype(jnp.bfloat16)
        for which in range(2):
            finals[which].start()
        for k in range(KVH):
            for which in range(2):
                store(which, k).wait()
                for dst in range(m + 1, n):
                    send_kv(which, k, m, dst).wait_send()
                for dst in range(m):
                    send_part(which, k, m, dst).wait_send()
        for which in range(2):
            finals[which].wait()

    for m in range(n):
        pl.when(me == m)(functools.partial(on_device, m))


def write_out(*refs):
    sources, targets, sem = refs[:4], refs[4:8], refs[8]
    copies = []
    for index in range(4):
        pieces = 4 if index < 2 else 1
        step = sources[index].shape[0] // pieces
        for piece in range(pieces):
            part = pl.ds(piece * step, step)
            copies.append(
                pltpu.make_async_copy(
                    sources[index].at[part], targets[index].at[part], sem.at[index, piece]
                )
            )
    for copy in copies:
        copy.start()
    for copy in copies:
        copy.wait()


def shards(n, queries, keys, values, lengths, out_grad):
    rows = queries.shape[0]
    segs = lengths.shape[1]
    total = n * rows
    bf16 = jnp.bfloat16
    dma = pltpu.SemaphoreType.DMA
    wide = jax.ShapeDtypeStruct(queries.shape, bf16)
    thin = jax.ShapeDtypeStruct(keys.shape, bf16)
    anywhere = pl.BlockSpec(memory_space=pl.ANY)
    held = pl.pallas_call(
        functools.partial(kernel, n, rows, segs),
        out_shape=(wide, wide, thin, thin),
        in_specs=[pl.BlockSpec(memory_space=pltpu.HBM)] * 5,
        out_specs=(anywhere,) * 4,
        scratch_shapes=[
            pltpu.SMEM(lengths.shape, jnp.int32),
            pltpu.VMEM((rows, H * HD), bf16),
            pltpu.VMEM((rows, H * HD), bf16),
            pltpu.VMEM((HD, H * rows), bf16),
            pltpu.VMEM((HD, H * rows), bf16),
            pltpu.VMEM((rows, H * HD), bf16),
            pltpu.VMEM((rows, H * HD), bf16),
            pltpu.VMEM((rows, total), jnp.float32),
            pltpu.VMEM((2, total, KVH * HD), bf16),
            pltpu.VMEM((2, total, KVH * HD), bf16),
            pltpu.VMEM((2, total, KVH * HD), bf16),
            pltpu.VMEM((2, rows, KVH * HD), bf16),
            dma(()),
            dma((2, KVH)),
            dma((2,)),
            dma((2, KVH)),
            dma((2,)),
            dma((2, KVH, n)),
            dma((2, KVH, n)),
            dma((2, KVH, n)),
            dma((2, KVH, n)),
        ],
        compiler_params=pltpu.CompilerParams(
            collective_id=0, has_side_effects=True, vmem_limit_bytes=48 * 1024 * 1024
        ),
    )(*(
        pltpu.with_memory_space_constraint(x, pltpu.HBM)
        for x in (lengths, queries, keys, values, out_grad)
    ))
    return pl.pallas_call(
        write_out,
        out_shape=(wide, wide, thin, thin),
        in_specs=[anywhere] * 4,
        out_specs=(pl.BlockSpec(memory_space=pltpu.HBM),) * 4,
        scratch_shapes=[dma((4, 4))],
    )(*held)


def solution(mesh):
    rows = P(("dp", "seq"), None)
    return jax.shard_map(
        functools.partial(shards, mesh.shape["seq"]),
        mesh=mesh,
        in_specs=(rows, rows, rows, P("dp", None), rows),
        out_specs=(rows,) * 4,
        check_vma=False,
    )
```

```python
import functools

import jax
import jax.numpy as jnp
from jax import lax
from jax.experimental import pallas as pl
from jax.experimental.pallas import tpu as pltpu
from jax.sharding import PartitionSpec as P

H = 32
KVH = 4
HD = 128
GROUP = 8
SCALE = HD ** (-0.5)
EXP2_SCALE = SCALE * 1.4426950408889634
NT = (((1,), (1,)), ((), ()))
NN = (((1,), (0,)), ((), ()))


def dot(a, b, dims):
    return lax.dot_general(a, b, dims, preferred_element_type=jnp.float32)


def lanes(index, width):
    return pl.ds(pl.multiple_of(index * width, 128), width)


def kernel(
    n, rows, segs,
    lens_in, q_in, k_in, v_in, g_in,
    att_out, dq_out, dk_out, dv_out,
    lens, q, g, qt, gt, att, dq, bias,
    kv, part, got, own,
    lens_sem, load_sem, own_sem, store_sem, final_sem,
    kv_send, kv_recv, part_send, part_recv,
):
    me = lax.axis_index("seq")
    lens_copy = pltpu.make_async_copy(lens_in, lens, lens_sem)
    lens_copy.start()
    barrier = pltpu.get_barrier_semaphore()
    for step in range(1, n):
        pl.semaphore_signal(
            barrier, inc=1, device_id={"seq": lax.rem(me + step, n)},
            device_id_type=pl.DeviceIdType.MESH,
        )

    wide = GROUP * HD
    sources = (k_in, v_in)

    def load(which, k):
        return pltpu.make_async_copy(
            (q_in, g_in)[which].at[:, lanes(k, wide)],
            (q, g)[which].at[:, lanes(k, wide)],
            load_sem.at[which, k],
        )

    def store(which, k):
        return pltpu.make_async_copy(
            (att, dq)[which].at[:, lanes(k, wide)],
            (att_out, dq_out)[which].at[:, lanes(k, wide)],
            store_sem.at[which, k],
        )

    def send_kv(which, k, src, dst):
        return pltpu.make_async_remote_copy(
            src_ref=sources[which].at[:, lanes(k, HD)],
            dst_ref=kv.at[which, pl.ds(src * rows, rows), lanes(k, HD)],
            send_sem=kv_send.at[which, k, dst],
            recv_sem=kv_recv.at[which, k, src],
            device_id={"seq": dst},
            device_id_type=pl.DeviceIdType.MESH,
        )

    def send_part(which, k, src, dst):
        return pltpu.make_async_remote_copy(
            src_ref=part.at[which, pl.ds(dst * rows, rows), lanes(k, HD)],
            dst_ref=got.at[which, pl.ds(src * rows, rows), lanes(k, HD)],
            send_sem=part_send.at[which, k, dst],
            recv_sem=part_recv.at[which, k, src],
            device_id={"seq": dst},
            device_id_type=pl.DeviceIdType.MESH,
        )

    def on_device(m):
        length = (m + 1) * rows
        heads = GROUP
        while heads > 1 and heads * rows * length > 1 << 18:
            heads //= 2

        own_copies = [
            pltpu.make_async_copy(
                sources[which], kv.at[which, pl.ds(m * rows, rows), :], own_sem.at[which]
            )
            for which in range(2)
        ]
        for which in range(2):
            own_copies[which].start()
        for k in range(KVH):
            load(0, k).start()
            load(1, k).start()
        pl.semaphore_wait(barrier, n - 1)
        for k in range(KVH):
            for dst in range(m + 1, n):
                send_kv(0, k, m, dst).start()
                send_kv(1, k, m, dst).start()

        lens_copy.wait()
        pos = lax.broadcasted_iota(jnp.int32, (rows, 128), 0) + m * rows
        first = jnp.zeros((rows, 128), jnp.int32)
        end = jnp.int32(0)
        for seg in range(segs):
            end = end + lens[0, seg]
            first = jnp.maximum(first, jnp.where(pos >= end, end, 0))
        for c in range(length // 128):
            col = lax.broadcasted_iota(jnp.int32, (rows, 128), 1) + c * 128
            seen = (col >= first) & (col <= pos)
            bias[:, c * 128:(c + 1) * 128] = jnp.where(seen, 0.0, -1e30)

        @pl.loop(0, KVH)
        def _(k):
            load(0, k).wait()
            load(1, k).wait()
            for h in range(GROUP):
                head = k * GROUP + h
                qt[:, lanes(head, rows)] = q[:, lanes(head, HD)].T
                gt[:, lanes(head, rows)] = g[:, lanes(head, HD)].T

        for which in range(2):
            own_copies[which].wait()

        @pl.loop(0, KVH)
        def _(k):
            for src in range(m):
                send_kv(0, k, src, src).wait_recv()
                send_kv(1, k, src, src).wait_recv()
            key = kv[0, 0:length, lanes(k, HD)]
            value = kv[1, 0:length, lanes(k, HD)]
            dkt = jnp.zeros((HD, length), jnp.float32)
            dvt = jnp.zeros((HD, length), jnp.float32)
            for base in range(0, GROUP, heads):
                ids = [k * GROUP + base + h for h in range(heads)]
                qs = jnp.concatenate([q[:, lanes(i, HD)] for i in ids], axis=0)
                gs = jnp.concatenate([g[:, lanes(i, HD)] for i in ids], axis=0)
                raw = dot(qs, key, NT).reshape(heads, rows, length)
                raw = (raw + bias[:, 0:length][None]).reshape(heads * rows, length)
                top = jnp.max(raw, axis=-1, keepdims=True)
                expo = jnp.exp2((raw - top) * EXP2_SCALE)
                inv = 1.0 / jnp.sum(expo, axis=-1, keepdims=True)
                out = (dot(expo.astype(jnp.bfloat16), value, NN) * inv).astype(jnp.bfloat16)
                rowdot = jnp.sum(
                    gs.astype(jnp.float32) * out.astype(jnp.float32), axis=-1, keepdims=True
                )
                probs = expo * inv
                dscores = (probs * (dot(gs, value, NT) - rowdot)).astype(jnp.bfloat16)
                grad = (dot(dscores, key, NN) * SCALE).astype(jnp.bfloat16)
                for h in range(heads):
                    att[:, lanes(ids[h], HD)] = out[h * rows:(h + 1) * rows]
                    dq[:, lanes(ids[h], HD)] = grad[h * rows:(h + 1) * rows]
                span = pl.ds(pl.multiple_of(ids[0] * rows, 128), heads * rows)
                dkt += dot(qt[:, span], dscores, NN)
                dvt += dot(gt[:, span], probs.astype(jnp.bfloat16), NN)
            part[0, 0:length, lanes(k, HD)] = (dkt.T * SCALE).astype(jnp.bfloat16)
            part[1, 0:length, lanes(k, HD)] = dvt.T.astype(jnp.bfloat16)
            for dst in range(m):
                send_part(0, k, m, dst).start()
                send_part(1, k, m, dst).start()
            store(0, k).start()
            store(1, k).start()

        mine = pl.ds(m * rows, rows)
        finals = []
        for which in range(2):
            final = part.at[which, mine, :]
            if m < n - 1:
                final = own.at[which]
            finals.append(
                pltpu.make_async_copy(final, (dk_out, dv_out)[which], final_sem.at[which])
            )
        if m < n - 1:
            for k in range(KVH):
                for which in range(2):
                    total = part[which, mine, lanes(k, HD)].astype(jnp.float32)
                    for src in range(m + 1, n):
                        send_part(which, k, src, src).wait_recv()
                        total += got[which, pl.ds(src * rows, rows), lanes(k, HD)].astype(
                            jnp.float32
                        )
                    own[which, :, lanes(k, HD)] = total.astype(jnp.bfloat16)
        for which in range(2):
            finals[which].start()
        for k in range(KVH):
            for which in range(2):
                store(which, k).wait()
                for dst in range(m + 1, n):
                    send_kv(which, k, m, dst).wait_send()
                for dst in range(m):
                    send_part(which, k, m, dst).wait_send()
        for which in range(2):
            finals[which].wait()

    for m in range(n):
        pl.when(me == m)(functools.partial(on_device, m))


def write_out(*refs):
    sources, targets, sem = refs[:4], refs[4:8], refs[8]
    copies = []
    for index in range(4):
        pieces = 4 if index < 2 else 1
        step = sources[index].shape[0] // pieces
        for piece in range(pieces):
            part = pl.ds(piece * step, step)
            copies.append(
                pltpu.make_async_copy(
                    sources[index].at[part], targets[index].at[part], sem.at[index, piece]
                )
            )
    for copy in copies:
        copy.start()
    for copy in copies:
        copy.wait()


def shards(n, queries, keys, values, lengths, out_grad):
    rows = queries.shape[0]
    segs = lengths.shape[1]
    total = n * rows
    bf16 = jnp.bfloat16
    dma = pltpu.SemaphoreType.DMA
    wide = jax.ShapeDtypeStruct(queries.shape, bf16)
    thin = jax.ShapeDtypeStruct(keys.shape, bf16)
    anywhere = pl.BlockSpec(memory_space=pl.ANY)
    held = pl.pallas_call(
        functools.partial(kernel, n, rows, segs),
        out_shape=(wide, wide, thin, thin),
        in_specs=[pl.BlockSpec(memory_space=pltpu.HBM)] * 5,
        out_specs=(anywhere,) * 4,
        scratch_shapes=[
            pltpu.SMEM(lengths.shape, jnp.int32),
            pltpu.VMEM((rows, H * HD), bf16),
            pltpu.VMEM((rows, H * HD), bf16),
            pltpu.VMEM((HD, H * rows), bf16),
            pltpu.VMEM((HD, H * rows), bf16),
            pltpu.VMEM((rows, H * HD), bf16),
            pltpu.VMEM((rows, H * HD), bf16),
            pltpu.VMEM((rows, total), jnp.float32),
            pltpu.VMEM((2, total, KVH * HD), bf16),
            pltpu.VMEM((2, total, KVH * HD), bf16),
            pltpu.VMEM((2, total, KVH * HD), bf16),
            pltpu.VMEM((2, rows, KVH * HD), bf16),
            dma(()),
            dma((2, KVH)),
            dma((2,)),
            dma((2, KVH)),
            dma((2,)),
            dma((2, KVH, n)),
            dma((2, KVH, n)),
            dma((2, KVH, n)),
            dma((2, KVH, n)),
        ],
        compiler_params=pltpu.CompilerParams(
            collective_id=0, has_side_effects=True, vmem_limit_bytes=48 * 1024 * 1024
        ),
    )(*(
        pltpu.with_memory_space_constraint(x, pltpu.HBM)
        for x in (lengths, queries, keys, values, out_grad)
    ))
    return pl.pallas_call(
        write_out,
        out_shape=(wide, wide, thin, thin),
        in_specs=[anywhere] * 4,
        out_specs=(pl.BlockSpec(memory_space=pltpu.HBM),) * 4,
        scratch_shapes=[dma((4, 4))],
        compiler_params=pltpu.CompilerParams(vmem_limit_bytes=1024 * 1024),
    )(*(pltpu.with_memory_space_constraint(x, pltpu.VMEM) for x in held))


def solution(mesh):
    rows = P(("dp", "seq"), None)
    return jax.shard_map(
        functools.partial(shards, mesh.shape["seq"]),
        mesh=mesh,
        in_specs=(rows, rows, rows, P("dp", None), rows),
        out_specs=(rows,) * 4,
        check_vma=False,
    )
```

```python
import functools

import jax
import jax.numpy as jnp
from jax import lax
from jax.experimental import pallas as pl
from jax.experimental.pallas import tpu as pltpu
from jax.sharding import PartitionSpec as P

H = 32
KVH = 4
HD = 128
GROUP = 8
SCALE = HD ** (-0.5)
EXP2_SCALE = SCALE * 1.4426950408889634
NT = (((1,), (1,)), ((), ()))
NN = (((1,), (0,)), ((), ()))


def dot(a, b, dims):
    return lax.dot_general(a, b, dims, preferred_element_type=jnp.float32)


def lanes(index, width):
    return pl.ds(pl.multiple_of(index * width, 128), width)


def kernel(
    n, rows, segs,
    lens_in, q_in, k_in, v_in, g_in,
    att, dq, dk, dv,
    lens, q, g, qt, gt, bias,
    kv, part, got,
    lens_sem, load_sem, own_sem,
    kv_send, kv_recv, part_send, part_recv,
):
    me = lax.axis_index("seq")
    lens_copy = pltpu.make_async_copy(lens_in, lens, lens_sem)
    lens_copy.start()
    barrier = pltpu.get_barrier_semaphore()
    for step in range(1, n):
        pl.semaphore_signal(
            barrier, inc=1, device_id={"seq": lax.rem(me + step, n)},
            device_id_type=pl.DeviceIdType.MESH,
        )

    wide = GROUP * HD
    sources = (k_in, v_in)

    def load(which, k):
        return pltpu.make_async_copy(
            (q_in, g_in)[which].at[:, lanes(k, wide)],
            (q, g)[which].at[:, lanes(k, wide)],
            load_sem.at[which, k],
        )

    def send_kv(which, k, src, dst):
        return pltpu.make_async_remote_copy(
            src_ref=sources[which].at[:, lanes(k, HD)],
            dst_ref=kv.at[which, pl.ds(src * rows, rows), lanes(k, HD)],
            send_sem=kv_send.at[which, k, dst],
            recv_sem=kv_recv.at[which, k, src],
            device_id={"seq": dst},
            device_id_type=pl.DeviceIdType.MESH,
        )

    def send_part(which, k, src, dst):
        return pltpu.make_async_remote_copy(
            src_ref=part.at[which, pl.ds(dst * rows, rows), lanes(k, HD)],
            dst_ref=got.at[which, pl.ds(src * rows, rows), lanes(k, HD)],
            send_sem=part_send.at[which, k, dst],
            recv_sem=part_recv.at[which, k, src],
            device_id={"seq": dst},
            device_id_type=pl.DeviceIdType.MESH,
        )

    def on_device(m):
        length = (m + 1) * rows
        heads = GROUP
        while heads > 1 and heads * rows * length > 1 << 16:
            heads //= 2

        own_copies = [
            pltpu.make_async_copy(
                sources[which], kv.at[which, pl.ds(m * rows, rows), :], own_sem.at[which]
            )
            for which in range(2)
        ]
        for which in range(2):
            own_copies[which].start()
        for k in range(KVH):
            load(0, k).start()
            load(1, k).start()
        pl.semaphore_wait(barrier, n - 1)
        for k in range(KVH):
            for dst in range(m + 1, n):
                send_kv(0, k, m, dst).start()
                send_kv(1, k, m, dst).start()

        lens_copy.wait()
        pos = lax.broadcasted_iota(jnp.int32, (rows, 128), 0) + m * rows
        first = jnp.zeros((rows, 128), jnp.int32)
        end = jnp.int32(0)
        for seg in range(segs):
            end = end + lens[0, seg]
            first = jnp.maximum(first, jnp.where(pos >= end, end, 0))
        for c in range(length // 128):
            col = lax.broadcasted_iota(jnp.int32, (rows, 128), 1) + c * 128
            seen = (col >= first) & (col <= pos)
            bias[:, c * 128:(c + 1) * 128] = jnp.where(seen, 0.0, -1e30)

        @pl.loop(0, KVH)
        def _(k):
            load(0, k).wait()
            load(1, k).wait()
            for h in range(GROUP):
                head = k * GROUP + h
                qt[:, lanes(head, rows)] = q[:, lanes(head, HD)].T
                gt[:, lanes(head, rows)] = g[:, lanes(head, HD)].T

        for which in range(2):
            own_copies[which].wait()

        @pl.loop(0, KVH)
        def _(k):
            for src in range(m):
                send_kv(0, k, src, src).wait_recv()
                send_kv(1, k, src, src).wait_recv()
            key = kv[0, 0:length, lanes(k, HD)]
            value = kv[1, 0:length, lanes(k, HD)]
            dkt = jnp.zeros((HD, length), jnp.float32)
            dvt = jnp.zeros((HD, length), jnp.float32)
            for base in range(0, GROUP, heads):
                ids = [k * GROUP + base + h for h in range(heads)]
                qs = jnp.concatenate([q[:, lanes(i, HD)] for i in ids], axis=0)
                gs = jnp.concatenate([g[:, lanes(i, HD)] for i in ids], axis=0)
                raw = dot(qs, key, NT).reshape(heads, rows, length)
                raw = (raw + bias[:, 0:length][None]).reshape(heads * rows, length)
                top = jnp.max(raw, axis=-1, keepdims=True)
                expo = jnp.exp2((raw - top) * EXP2_SCALE)
                inv = 1.0 / jnp.sum(expo, axis=-1, keepdims=True)
                out = (dot(expo.astype(jnp.bfloat16), value, NN) * inv).astype(jnp.bfloat16)
                rowdot = jnp.sum(
                    gs.astype(jnp.float32) * out.astype(jnp.float32), axis=-1, keepdims=True
                )
                probs = expo * inv
                dscores = (probs * (dot(gs, value, NT) - rowdot)).astype(jnp.bfloat16)
                grad = (dot(dscores, key, NN) * SCALE).astype(jnp.bfloat16)
                for h in range(heads):
                    att[:, lanes(ids[h], HD)] = out[h * rows:(h + 1) * rows]
                    dq[:, lanes(ids[h], HD)] = grad[h * rows:(h + 1) * rows]
                span = pl.ds(pl.multiple_of(ids[0] * rows, 128), heads * rows)
                dkt += dot(qt[:, span], dscores, NN)
                dvt += dot(gt[:, span], probs.astype(jnp.bfloat16), NN)
            part[0, 0:length, lanes(k, HD)] = (dkt.T * SCALE).astype(jnp.bfloat16)
            part[1, 0:length, lanes(k, HD)] = dvt.T.astype(jnp.bfloat16)
            for dst in range(m):
                send_part(0, k, m, dst).start()
                send_part(1, k, m, dst).start()

        mine = pl.ds(m * rows, rows)
        if m < n - 1:
            for k in range(KVH):
                for which in range(2):
                    total = part[which, mine, lanes(k, HD)].astype(jnp.float32)
                    for src in range(m + 1, n):
                        send_part(which, k, src, src).wait_recv()
                        total += got[which, pl.ds(src * rows, rows), lanes(k, HD)].astype(
                            jnp.float32
                        )
                    (dk, dv)[which][:, lanes(k, HD)] = total.astype(jnp.bfloat16)
        else:
            dk[...] = part[0, mine, :]
            dv[...] = part[1, mine, :]
        for k in range(KVH):
            for which in range(2):
                for dst in range(m + 1, n):
                    send_kv(which, k, m, dst).wait_send()
                for dst in range(m):
                    send_part(which, k, m, dst).wait_send()

    for m in range(n):
        pl.when(me == m)(functools.partial(on_device, m))


def write_out(*refs):
    sources, targets, sem = refs[:4], refs[4:8], refs[8]
    copies = []
    for index in range(4):
        pieces = 4 if index < 2 else 1
        step = sources[index].shape[0] // pieces
        for piece in range(pieces):
            part = pl.ds(piece * step, step)
            copies.append(
                pltpu.make_async_copy(
                    sources[index].at[part], targets[index].at[part], sem.at[index, piece]
                )
            )
    for copy in copies:
        copy.start()
    for copy in copies:
        copy.wait()


def shards(n, queries, keys, values, lengths, out_grad):
    rows = queries.shape[0]
    segs = lengths.shape[1]
    total = n * rows
    bf16 = jnp.bfloat16
    dma = pltpu.SemaphoreType.DMA
    wide = jax.ShapeDtypeStruct(queries.shape, bf16)
    thin = jax.ShapeDtypeStruct(keys.shape, bf16)
    anywhere = pl.BlockSpec(memory_space=pl.ANY)
    held = pl.pallas_call(
        functools.partial(kernel, n, rows, segs),
        out_shape=tuple(pltpu.VMEM(x.shape, bf16) for x in (wide, wide, thin, thin)),
        in_specs=[pl.BlockSpec(memory_space=pltpu.HBM)] * 5,
        out_specs=(pl.BlockSpec(memory_space=pltpu.VMEM),) * 4,
        scratch_shapes=[
            pltpu.SMEM(lengths.shape, jnp.int32),
            pltpu.VMEM((rows, H * HD), bf16),
            pltpu.VMEM((rows, H * HD), bf16),
            pltpu.VMEM((HD, H * rows), bf16),
            pltpu.VMEM((HD, H * rows), bf16),
            pltpu.VMEM((rows, total), jnp.float32),
            pltpu.VMEM((2, total, KVH * HD), bf16),
            pltpu.VMEM((2, total, KVH * HD), bf16),
            pltpu.VMEM((2, total, KVH * HD), bf16),
            dma(()),
            dma((2, KVH)),
            dma((2,)),
            dma((2, KVH, n)),
            dma((2, KVH, n)),
            dma((2, KVH, n)),
            dma((2, KVH, n)),
        ],
        compiler_params=pltpu.CompilerParams(
            collective_id=0, has_side_effects=True, vmem_limit_bytes=48 * 1024 * 1024
        ),
    )(*(
        pltpu.with_memory_space_constraint(x, pltpu.HBM)
        for x in (lengths, queries, keys, values, out_grad)
    ))
    return pl.pallas_call(
        write_out,
        out_shape=(wide, wide, thin, thin),
        in_specs=[anywhere] * 4,
        out_specs=(pl.BlockSpec(memory_space=pltpu.HBM),) * 4,
        scratch_shapes=[dma((4, 4))],
        compiler_params=pltpu.CompilerParams(vmem_limit_bytes=1024 * 1024),
    )(*(pltpu.with_memory_space_constraint(x, pltpu.VMEM) for x in held))


def solution(mesh):
    rows = P(("dp", "seq"), None)
    return jax.shard_map(
        functools.partial(shards, mesh.shape["seq"]),
        mesh=mesh,
        in_specs=(rows, rows, rows, P("dp", None), rows),
        out_specs=(rows,) * 4,
        check_vma=False,
    )
```

```python
import functools

import jax
import jax.numpy as jnp
from jax import lax
from jax.experimental import pallas as pl
from jax.experimental.pallas import tpu as pltpu
from jax.sharding import PartitionSpec as P

H = 32
KVH = 4
HD = 128
GROUP = 8
SCALE = HD ** (-0.5)
EXP2_SCALE = SCALE * 1.4426950408889634
NT = (((1,), (1,)), ((), ()))
NN = (((1,), (0,)), ((), ()))


def dot(a, b, dims):
    return lax.dot_general(a, b, dims, preferred_element_type=jnp.float32)


def lanes(index, width):
    return pl.ds(pl.multiple_of(index * width, 128), width)


def stacked(ref, first, count):
    return jnp.concatenate([ref[:, lanes(first + h, HD)] for h in range(count)], axis=0)


def kernel(
    n, rows, segs,
    lens_in, q_in, k_in, v_in, g_in,
    att, dq, dk, dv,
    lens, q, g, qt, gt, bias,
    kv, part, got,
    lens_sem, load_sem, own_sem,
    kv_send, kv_recv, part_send, part_recv,
):
    me = lax.axis_index("seq")
    lens_copy = pltpu.make_async_copy(lens_in, lens, lens_sem)
    lens_copy.start()
    barrier = pltpu.get_barrier_semaphore()
    for step in range(1, n):
        pl.semaphore_signal(
            barrier, inc=1, device_id={"seq": lax.rem(me + step, n)},
            device_id_type=pl.DeviceIdType.MESH,
        )

    wide = GROUP * HD
    sources = (k_in, v_in)

    def load(which, k):
        return pltpu.make_async_copy(
            (q_in, g_in)[which].at[:, lanes(k, wide)],
            (q, g)[which].at[:, lanes(k, wide)],
            load_sem.at[which, k],
        )

    def send_kv(which, k, src, dst):
        return pltpu.make_async_remote_copy(
            src_ref=sources[which].at[:, lanes(k, HD)],
            dst_ref=kv.at[which, pl.ds(src * rows, rows), lanes(k, HD)],
            send_sem=kv_send.at[which, k, dst],
            recv_sem=kv_recv.at[which, k, src],
            device_id={"seq": dst},
            device_id_type=pl.DeviceIdType.MESH,
        )

    def send_part(which, k, src, dst):
        return pltpu.make_async_remote_copy(
            src_ref=part.at[which, pl.ds(dst * rows, rows), lanes(k, HD)],
            dst_ref=got.at[which, pl.ds(src * rows, rows), lanes(k, HD)],
            send_sem=part_send.at[which, k, dst],
            recv_sem=part_recv.at[which, k, src],
            device_id={"seq": dst},
            device_id_type=pl.DeviceIdType.MESH,
        )

    def on_device(m):
        length = (m + 1) * rows
        heads = GROUP
        while heads > 1 and heads * rows * length > 1 << 18:
            heads //= 2

        own_copies = [
            pltpu.make_async_copy(
                sources[which], kv.at[which, pl.ds(m * rows, rows), :], own_sem.at[which]
            )
            for which in range(2)
        ]
        for which in range(2):
            own_copies[which].start()
        for k in range(KVH):
            load(0, k).start()
            load(1, k).start()
        pl.semaphore_wait(barrier, n - 1)
        for k in range(KVH):
            for dst in range(m + 1, n):
                send_kv(0, k, m, dst).start()
                send_kv(1, k, m, dst).start()

        lens_copy.wait()
        pos = lax.broadcasted_iota(jnp.int32, (rows, 128), 0) + m * rows
        first = jnp.zeros((rows, 128), jnp.int32)
        end = jnp.int32(0)
        for seg in range(segs):
            end = end + lens[0, seg]
            first = jnp.maximum(first, jnp.where(pos >= end, end, 0))
        for c in range(length // 128):
            col = lax.broadcasted_iota(jnp.int32, (rows, 128), 1) + c * 128
            seen = (col >= first) & (col <= pos)
            bias[:, c * 128:(c + 1) * 128] = jnp.where(seen, 0.0, -1e30)

        @pl.loop(0, KVH)
        def _(k):
            load(0, k).wait()
            load(1, k).wait()
            for h in range(GROUP):
                head = k * GROUP + h
                qt[:, lanes(head, rows)] = q[:, lanes(head, HD)].T
                gt[:, lanes(head, rows)] = g[:, lanes(head, HD)].T

        for which in range(2):
            own_copies[which].wait()

        @pl.loop(0, KVH)
        def _(k):
            for src in range(m):
                send_kv(0, k, src, src).wait_recv()
                send_kv(1, k, src, src).wait_recv()
            key = kv[0, 0:length, lanes(k, HD)]
            value = kv[1, 0:length, lanes(k, HD)]
            dkt = jnp.zeros((HD, length), jnp.float32)
            dvt = jnp.zeros((HD, length), jnp.float32)
            ones = jnp.ones((length, HD), jnp.bfloat16)
            value_ones = jnp.concatenate([value, ones], axis=1)
            piece = max(1, heads // 2)
            grads = []
            for base in range(0, GROUP, heads):
                firsts = [k * GROUP + base + p for p in range(0, heads, piece)]
                qs, gs, raws, dprobs, expos, weighted = [], [], [], [], [], []
                for i in firsts:
                    qs.append(stacked(q, i, piece))
                    gs.append(stacked(g, i, piece))
                    raws.append(dot(qs[-1], key, NT))
                for p in range(len(firsts)):
                    dprobs.append(dot(gs[p], value, NT))
                    raw = raws[p].reshape(piece, rows, length) + bias[:, 0:length][None]
                    raw = raw.reshape(piece * rows, length)
                    top = jnp.max(raw, axis=-1, keepdims=True)
                    expos.append(jnp.exp2((raw - top) * EXP2_SCALE))
                    weighted.append(dot(expos[-1].astype(jnp.bfloat16), value_ones, NN))
                for p, i in enumerate(firsts):
                    inv = 1.0 / weighted[p][:, HD:]
                    out = (weighted[p][:, :HD] * inv).astype(jnp.bfloat16)
                    for h in range(piece):
                        att[:, lanes(i + h, HD)] = out[h * rows:(h + 1) * rows]
                    rowdot = jnp.sum(
                        gs[p].astype(jnp.float32) * out.astype(jnp.float32),
                        axis=-1, keepdims=True,
                    )
                    probs = expos[p] * jnp.concatenate([inv] * (length // HD), axis=1)
                    dscores = (probs * (dprobs[p] - rowdot)).astype(jnp.bfloat16)
                    span = pl.ds(pl.multiple_of(i * rows, 128), piece * rows)
                    dvt += dot(gt[:, span], probs.astype(jnp.bfloat16), NN)
                    dkt += dot(qt[:, span], dscores, NN)
                    grads.append((i, dscores))
            part[1, 0:length, lanes(k, HD)] = dvt.T.astype(jnp.bfloat16)
            part[0, 0:length, lanes(k, HD)] = (dkt.T * SCALE).astype(jnp.bfloat16)
            for dst in range(m):
                send_part(0, k, m, dst).start()
                send_part(1, k, m, dst).start()
            for i, dscores in grads:
                grad = (dot(dscores, key, NN) * SCALE).astype(jnp.bfloat16)
                for h in range(piece):
                    dq[:, lanes(i + h, HD)] = grad[h * rows:(h + 1) * rows]

        mine = pl.ds(m * rows, rows)
        if m < n - 1:
            for k in range(KVH):
                for which in range(2):
                    total = part[which, mine, lanes(k, HD)].astype(jnp.float32)
                    for src in range(m + 1, n):
                        send_part(which, k, src, src).wait_recv()
                        total += got[which, pl.ds(src * rows, rows), lanes(k, HD)].astype(
                            jnp.float32
                        )
                    (dk, dv)[which][:, lanes(k, HD)] = total.astype(jnp.bfloat16)
        else:
            dk[...] = part[0, mine, :]
            dv[...] = part[1, mine, :]
        for k in range(KVH):
            for which in range(2):
                for dst in range(m + 1, n):
                    send_kv(which, k, m, dst).wait_send()
                for dst in range(m):
                    send_part(which, k, m, dst).wait_send()

    for m in range(n):
        pl.when(me == m)(functools.partial(on_device, m))


def write_out(*refs):
    sources, targets, sem = refs[:4], refs[4:8], refs[8]
    copies = []
    for index in range(4):
        pieces = 4 if index < 2 else 1
        step = sources[index].shape[0] // pieces
        for piece in range(pieces):
            part = pl.ds(piece * step, step)
            copies.append(
                pltpu.make_async_copy(
                    sources[index].at[part], targets[index].at[part], sem.at[index, piece]
                )
            )
    for copy in copies:
        copy.start()
    for copy in copies:
        copy.wait()


def shards(n, queries, keys, values, lengths, out_grad):
    rows = queries.shape[0]
    segs = lengths.shape[1]
    total = n * rows
    bf16 = jnp.bfloat16
    dma = pltpu.SemaphoreType.DMA
    wide = jax.ShapeDtypeStruct(queries.shape, bf16)
    thin = jax.ShapeDtypeStruct(keys.shape, bf16)
    anywhere = pl.BlockSpec(memory_space=pl.ANY)
    held = pl.pallas_call(
        functools.partial(kernel, n, rows, segs),
        out_shape=tuple(pltpu.VMEM(x.shape, bf16) for x in (wide, wide, thin, thin)),
        in_specs=[pl.BlockSpec(memory_space=pltpu.HBM)] * 5,
        out_specs=(pl.BlockSpec(memory_space=pltpu.VMEM),) * 4,
        scratch_shapes=[
            pltpu.SMEM(lengths.shape, jnp.int32),
            pltpu.VMEM((rows, H * HD), bf16),
            pltpu.VMEM((rows, H * HD), bf16),
            pltpu.VMEM((HD, H * rows), bf16),
            pltpu.VMEM((HD, H * rows), bf16),
            pltpu.VMEM((rows, total), jnp.float32),
            pltpu.VMEM((2, total, KVH * HD), bf16),
            pltpu.VMEM((2, total, KVH * HD), bf16),
            pltpu.VMEM((2, total, KVH * HD), bf16),
            dma(()),
            dma((2, KVH)),
            dma((2,)),
            dma((2, KVH, n)),
            dma((2, KVH, n)),
            dma((2, KVH, n)),
            dma((2, KVH, n)),
        ],
        compiler_params=pltpu.CompilerParams(
            collective_id=0, has_side_effects=True, vmem_limit_bytes=48 * 1024 * 1024
        ),
    )(*(
        pltpu.with_memory_space_constraint(x, pltpu.HBM)
        for x in (lengths, queries, keys, values, out_grad)
    ))
    return pl.pallas_call(
        write_out,
        out_shape=(wide, wide, thin, thin),
        in_specs=[anywhere] * 4,
        out_specs=(pl.BlockSpec(memory_space=pltpu.HBM),) * 4,
        scratch_shapes=[dma((4, 4))],
        compiler_params=pltpu.CompilerParams(vmem_limit_bytes=1024 * 1024),
    )(*(pltpu.with_memory_space_constraint(x, pltpu.VMEM) for x in held))


def solution(mesh):
    rows = P(("dp", "seq"), None)
    return jax.shard_map(
        functools.partial(shards, mesh.shape["seq"]),
        mesh=mesh,
        in_specs=(rows, rows, rows, P("dp", None), rows),
        out_specs=(rows,) * 4,
        check_vma=False,
    )
```

```python
import functools

import jax
import jax.numpy as jnp
from jax import lax
from jax.experimental import pallas as pl
from jax.experimental.pallas import tpu as pltpu
from jax.sharding import PartitionSpec as P

H = 32
KVH = 4
HD = 128
GROUP = 8
SCALE = HD ** (-0.5)
EXP2_SCALE = SCALE * 1.4426950408889634
NT = (((1,), (1,)), ((), ()))
NN = (((1,), (0,)), ((), ()))


def dot(a, b, dims):
    return lax.dot_general(a, b, dims, preferred_element_type=jnp.float32)


def lanes(index, width):
    return pl.ds(pl.multiple_of(index * width, 128), width)


def stacked(ref, first, count):
    return jnp.concatenate([ref[:, lanes(first + h, HD)] for h in range(count)], axis=0)


def kernel(
    n, rows, segs,
    lens_in, q_in, k_in, v_in, g_in,
    att, dq, dk, dv,
    lens, q, g, qt, gt, kept, bias,
    kv, part, got,
    lens_sem, load_sem, own_sem,
    kv_send, kv_recv, part_send, part_recv,
):
    me = lax.axis_index("seq")
    lens_copy = pltpu.make_async_copy(lens_in, lens, lens_sem)
    lens_copy.start()
    barrier = pltpu.get_barrier_semaphore()
    for step in range(1, n):
        pl.semaphore_signal(
            barrier, inc=1, device_id={"seq": lax.rem(me + step, n)},
            device_id_type=pl.DeviceIdType.MESH,
        )

    wide = GROUP * HD
    sources = (k_in, v_in)

    def load(which, k):
        return pltpu.make_async_copy(
            (q_in, g_in)[which].at[:, lanes(k, wide)],
            (q, g)[which].at[:, lanes(k, wide)],
            load_sem.at[which, k],
        )

    def send_kv(which, k, src, dst):
        return pltpu.make_async_remote_copy(
            src_ref=sources[which].at[:, lanes(k, HD)],
            dst_ref=kv.at[which, pl.ds(src * rows, rows), lanes(k, HD)],
            send_sem=kv_send.at[which, k, dst],
            recv_sem=kv_recv.at[which, k, src],
            device_id={"seq": dst},
            device_id_type=pl.DeviceIdType.MESH,
        )

    def send_part(which, k, src, dst):
        return pltpu.make_async_remote_copy(
            src_ref=part.at[which, pl.ds(dst * rows, rows), lanes(k, HD)],
            dst_ref=got.at[which, pl.ds(src * rows, rows), lanes(k, HD)],
            send_sem=part_send.at[which, k, dst],
            recv_sem=part_recv.at[which, k, src],
            device_id={"seq": dst},
            device_id_type=pl.DeviceIdType.MESH,
        )

    def on_device(m):
        length = (m + 1) * rows
        heads = GROUP
        while heads > 1 and heads * rows * length > 1 << 18:
            heads //= 2

        own_copies = [
            pltpu.make_async_copy(
                sources[which], kv.at[which, pl.ds(m * rows, rows), :], own_sem.at[which]
            )
            for which in range(2)
        ]
        for which in range(2):
            own_copies[which].start()
        for k in range(KVH):
            load(0, k).start()
            load(1, k).start()
        pl.semaphore_wait(barrier, n - 1)
        for k in range(KVH):
            for dst in range(m + 1, n):
                send_kv(0, k, m, dst).start()
                send_kv(1, k, m, dst).start()

        lens_copy.wait()
        pos = lax.broadcasted_iota(jnp.int32, (rows, 128), 0) + m * rows
        first = jnp.zeros((rows, 128), jnp.int32)
        end = jnp.int32(0)
        for seg in range(segs):
            end = end + lens[0, seg]
            first = jnp.maximum(first, jnp.where(pos >= end, end, 0))
        for c in range(length // 128):
            col = lax.broadcasted_iota(jnp.int32, (rows, 128), 1) + c * 128
            seen = (col >= first) & (col <= pos)
            bias[:, c * 128:(c + 1) * 128] = jnp.where(seen, 0.0, -1e30)

        @pl.loop(0, KVH)
        def _(k):
            load(0, k).wait()
            load(1, k).wait()
            for h in range(GROUP):
                head = k * GROUP + h
                qt[:, lanes(head, rows)] = q[:, lanes(head, HD)].T
                gt[:, lanes(head, rows)] = g[:, lanes(head, HD)].T

        for which in range(2):
            own_copies[which].wait()

        @pl.loop(0, KVH)
        def _(k):
            for src in range(m):
                send_kv(0, k, src, src).wait_recv()
                send_kv(1, k, src, src).wait_recv()
            key = kv[0, 0:length, lanes(k, HD)]
            value = kv[1, 0:length, lanes(k, HD)]
            dkt = jnp.zeros((HD, length), jnp.float32)
            dvt = jnp.zeros((HD, length), jnp.float32)
            ones = jnp.ones((length, HD), jnp.bfloat16)
            value_ones = jnp.concatenate([value, ones], axis=1)
            piece = max(1, heads // 2)
            for base in range(0, GROUP, heads):
                firsts = [k * GROUP + base + p for p in range(0, heads, piece)]
                qs, gs, raws, dprobs, expos, weighted = [], [], [], [], [], []
                for i in firsts:
                    qs.append(stacked(q, i, piece))
                    gs.append(stacked(g, i, piece))
                    raws.append(dot(qs[-1], key, NT))
                for p in range(len(firsts)):
                    dprobs.append(dot(gs[p], value, NT))
                    raw = raws[p].reshape(piece, rows, length) + bias[:, 0:length][None]
                    raw = raw.reshape(piece * rows, length)
                    top = jnp.max(raw, axis=-1, keepdims=True)
                    expos.append(jnp.exp2((raw - top) * EXP2_SCALE))
                    weighted.append(dot(expos[-1].astype(jnp.bfloat16), value_ones, NN))
                for p, i in enumerate(firsts):
                    inv = 1.0 / weighted[p][:, HD:]
                    out = (weighted[p][:, :HD] * inv).astype(jnp.bfloat16)
                    for h in range(piece):
                        att[:, lanes(i + h, HD)] = out[h * rows:(h + 1) * rows]
                    rowdot = jnp.sum(
                        gs[p].astype(jnp.float32) * out.astype(jnp.float32),
                        axis=-1, keepdims=True,
                    )
                    probs = expos[p] * jnp.concatenate([inv] * (length // HD), axis=1)
                    dscores = (probs * (dprobs[p] - rowdot)).astype(jnp.bfloat16)
                    span = pl.ds(pl.multiple_of(i * rows, 128), piece * rows)
                    dvt += dot(gt[:, span], probs.astype(jnp.bfloat16), NN)
                    dkt += dot(qt[:, span], dscores, NN)
                    kept[pl.ds(pl.multiple_of(i * rows, 128), piece * rows), 0:length] = dscores
            part[1, 0:length, lanes(k, HD)] = dvt.T.astype(jnp.bfloat16)
            part[0, 0:length, lanes(k, HD)] = (dkt.T * SCALE).astype(jnp.bfloat16)
            for dst in range(m):
                send_part(0, k, m, dst).start()
                send_part(1, k, m, dst).start()

        @pl.loop(0, KVH)
        def _(k):
            first = k * GROUP
            dscores = kept[pl.ds(pl.multiple_of(first * rows, 128), GROUP * rows), 0:length]
            grad = dot(dscores, kv[0, 0:length, lanes(k, HD)], NN) * SCALE
            for h in range(GROUP):
                dq[:, lanes(first + h, HD)] = grad[h * rows:(h + 1) * rows].astype(jnp.bfloat16)

        mine = pl.ds(m * rows, rows)
        if m < n - 1:
            for k in range(KVH):
                for which in range(2):
                    total = part[which, mine, lanes(k, HD)].astype(jnp.float32)
                    for src in range(m + 1, n):
                        send_part(which, k, src, src).wait_recv()
                        total += got[which, pl.ds(src * rows, rows), lanes(k, HD)].astype(
                            jnp.float32
                        )
                    (dk, dv)[which][:, lanes(k, HD)] = total.astype(jnp.bfloat16)
        else:
            dk[...] = part[0, mine, :]
            dv[...] = part[1, mine, :]
        for k in range(KVH):
            for which in range(2):
                for dst in range(m + 1, n):
                    send_kv(which, k, m, dst).wait_send()
                for dst in range(m):
                    send_part(which, k, m, dst).wait_send()

    for m in range(n):
        pl.when(me == m)(functools.partial(on_device, m))


def write_out(*refs):
    sources, targets, sem = refs[:4], refs[4:8], refs[8]
    copies = []
    for index in range(4):
        pieces = 4 if index < 2 else 1
        step = sources[index].shape[0] // pieces
        for piece in range(pieces):
            part = pl.ds(piece * step, step)
            copies.append(
                pltpu.make_async_copy(
                    sources[index].at[part], targets[index].at[part], sem.at[index, piece]
                )
            )
    for copy in copies:
        copy.start()
    for copy in copies:
        copy.wait()


def shards(n, queries, keys, values, lengths, out_grad):
    rows = queries.shape[0]
    segs = lengths.shape[1]
    total = n * rows
    bf16 = jnp.bfloat16
    dma = pltpu.SemaphoreType.DMA
    wide = jax.ShapeDtypeStruct(queries.shape, bf16)
    thin = jax.ShapeDtypeStruct(keys.shape, bf16)
    anywhere = pl.BlockSpec(memory_space=pl.ANY)
    held = pl.pallas_call(
        functools.partial(kernel, n, rows, segs),
        out_shape=tuple(pltpu.VMEM(x.shape, bf16) for x in (wide, wide, thin, thin)),
        in_specs=[pl.BlockSpec(memory_space=pltpu.HBM)] * 5,
        out_specs=(pl.BlockSpec(memory_space=pltpu.VMEM),) * 4,
        scratch_shapes=[
            pltpu.SMEM(lengths.shape, jnp.int32),
            pltpu.VMEM((rows, H * HD), bf16),
            pltpu.VMEM((rows, H * HD), bf16),
            pltpu.VMEM((HD, H * rows), bf16),
            pltpu.VMEM((HD, H * rows), bf16),
            pltpu.VMEM((H * rows, total), bf16),
            pltpu.VMEM((rows, total), jnp.float32),
            pltpu.VMEM((2, total, KVH * HD), bf16),
            pltpu.VMEM((2, total, KVH * HD), bf16),
            pltpu.VMEM((2, total, KVH * HD), bf16),
            dma(()),
            dma((2, KVH)),
            dma((2,)),
            dma((2, KVH, n)),
            dma((2, KVH, n)),
            dma((2, KVH, n)),
            dma((2, KVH, n)),
        ],
        compiler_params=pltpu.CompilerParams(
            collective_id=0, has_side_effects=True, vmem_limit_bytes=48 * 1024 * 1024
        ),
    )(*(
        pltpu.with_memory_space_constraint(x, pltpu.HBM)
        for x in (lengths, queries, keys, values, out_grad)
    ))
    return pl.pallas_call(
        write_out,
        out_shape=(wide, wide, thin, thin),
        in_specs=[anywhere] * 4,
        out_specs=(pl.BlockSpec(memory_space=pltpu.HBM),) * 4,
        scratch_shapes=[dma((4, 4))],
        compiler_params=pltpu.CompilerParams(vmem_limit_bytes=1024 * 1024),
    )(*(pltpu.with_memory_space_constraint(x, pltpu.VMEM) for x in held))


def solution(mesh):
    rows = P(("dp", "seq"), None)
    return jax.shard_map(
        functools.partial(shards, mesh.shape["seq"]),
        mesh=mesh,
        in_specs=(rows, rows, rows, P("dp", None), rows),
        out_specs=(rows,) * 4,
        check_vma=False,
    )
```

```python
import functools

import jax
import jax.numpy as jnp
from jax import lax
from jax.experimental import pallas as pl
from jax.experimental.pallas import tpu as pltpu
from jax.sharding import PartitionSpec as P

H = 32
KVH = 4
HD = 128
GROUP = 8
SCALE = HD ** (-0.5)
EXP2_SCALE = SCALE * 1.4426950408889634
NT = (((1,), (1,)), ((), ()))
NN = (((1,), (0,)), ((), ()))


def dot(a, b, dims):
    return lax.dot_general(a, b, dims, preferred_element_type=jnp.float32)


def lanes(index, width):
    return pl.ds(pl.multiple_of(index * width, 128), width)


def stacked(ref, first, count):
    return jnp.concatenate([ref[:, lanes(first + h, HD)] for h in range(count)], axis=0)


def kernel(
    n, rows, segs,
    lens_in, q_in, k_in, v_in, g_in,
    att, dq, dk, dv,
    lens, q, g, qt, gt, kept, bias,
    kv, part, got,
    lens_sem, load_sem, own_sem,
    kv_send, kv_recv, part_send, part_recv,
):
    me = lax.axis_index("seq")
    lens_copy = pltpu.make_async_copy(lens_in, lens, lens_sem)
    lens_copy.start()
    barrier = pltpu.get_barrier_semaphore()
    for step in range(1, n):
        pl.semaphore_signal(
            barrier, inc=1, device_id={"seq": lax.rem(me + step, n)},
            device_id_type=pl.DeviceIdType.MESH,
        )

    wide = GROUP * HD
    sources = (k_in, v_in)

    def load(which, k):
        return pltpu.make_async_copy(
            (q_in, g_in)[which].at[:, lanes(k, wide)],
            (q, g)[which].at[:, lanes(k, wide)],
            load_sem.at[which, k],
        )

    def send_kv(which, k, src, dst):
        return pltpu.make_async_remote_copy(
            src_ref=sources[which].at[:, lanes(k, HD)],
            dst_ref=kv.at[which, pl.ds(src * rows, rows), lanes(k, HD)],
            send_sem=kv_send.at[which, k, dst],
            recv_sem=kv_recv.at[which, k, src],
            device_id={"seq": dst},
            device_id_type=pl.DeviceIdType.MESH,
        )

    def send_part(which, k, src, dst):
        return pltpu.make_async_remote_copy(
            src_ref=part.at[which, pl.ds(dst * rows, rows), lanes(k, HD)],
            dst_ref=got.at[which, pl.ds(src * rows, rows), lanes(k, HD)],
            send_sem=part_send.at[which, k, dst],
            recv_sem=part_recv.at[which, k, src],
            device_id={"seq": dst},
            device_id_type=pl.DeviceIdType.MESH,
        )

    def on_device(m):
        length = (m + 1) * rows
        heads = GROUP
        while heads > 1 and heads * rows * length > 1 << 18:
            heads //= 2

        own_copies = [
            pltpu.make_async_copy(
                sources[which], kv.at[which, pl.ds(m * rows, rows), :], own_sem.at[which]
            )
            for which in range(2)
        ]
        for which in range(2):
            own_copies[which].start()
        for k in range(KVH):
            load(0, k).start()
            load(1, k).start()
        pl.semaphore_wait(barrier, n - 1)
        for k in range(KVH):
            for dst in range(m + 1, n):
                send_kv(0, k, m, dst).start()
                send_kv(1, k, m, dst).start()

        lens_copy.wait()
        pos = lax.broadcasted_iota(jnp.int32, (rows, 128), 0) + m * rows
        first = jnp.zeros((rows, 128), jnp.int32)
        end = jnp.int32(0)
        for seg in range(segs):
            end = end + lens[0, seg]
            first = jnp.maximum(first, jnp.where(pos >= end, end, 0))
        for c in range(length // 128):
            col = lax.broadcasted_iota(jnp.int32, (rows, 128), 1) + c * 128
            seen = (col >= first) & (col <= pos)
            bias[:, c * 128:(c + 1) * 128] = jnp.where(seen, 0.0, -1e30)

        @pl.loop(0, KVH)
        def _(k):
            load(0, k).wait()
            load(1, k).wait()
            for h in range(GROUP):
                head = k * GROUP + h
                qt[:, lanes(head, rows)] = q[:, lanes(head, HD)].T
                gt[:, lanes(head, rows)] = g[:, lanes(head, HD)].T

        for which in range(2):
            own_copies[which].wait()

        @pl.loop(0, KVH)
        def _(k):
            for src in range(m):
                send_kv(0, k, src, src).wait_recv()
                send_kv(1, k, src, src).wait_recv()
            key = kv[0, 0:length, lanes(k, HD)]
            value = kv[1, 0:length, lanes(k, HD)]
            dkt = jnp.zeros((HD, length), jnp.float32)
            dvt = jnp.zeros((HD, length), jnp.float32)
            ones = jnp.ones((length, HD), jnp.bfloat16)
            value_ones = jnp.concatenate([value, ones], axis=1)
            piece = max(1, heads // 4)
            for base in range(0, GROUP, heads):
                firsts = [k * GROUP + base + p for p in range(0, heads, piece)]
                qs, gs, raws, dprobs, expos, weighted = [], [], [], [], [], []
                for i in firsts:
                    qs.append(stacked(q, i, piece))
                    gs.append(stacked(g, i, piece))
                    raws.append(dot(qs[-1], key, NT))
                for p in range(len(firsts)):
                    dprobs.append(dot(gs[p], value, NT))
                    raw = raws[p].reshape(piece, rows, length) + bias[:, 0:length][None]
                    raw = raw.reshape(piece * rows, length)
                    top = jnp.max(raw, axis=-1, keepdims=True)
                    expos.append(jnp.exp2((raw - top) * EXP2_SCALE))
                    weighted.append(dot(expos[-1].astype(jnp.bfloat16), value_ones, NN))
                for p, i in enumerate(firsts):
                    inv = 1.0 / weighted[p][:, HD:]
                    out = (weighted[p][:, :HD] * inv).astype(jnp.bfloat16)
                    for h in range(piece):
                        att[:, lanes(i + h, HD)] = out[h * rows:(h + 1) * rows]
                    rowdot = jnp.sum(
                        gs[p].astype(jnp.float32) * out.astype(jnp.float32),
                        axis=-1, keepdims=True,
                    )
                    probs = expos[p] * jnp.concatenate([inv] * (length // HD), axis=1)
                    dscores = (probs * (dprobs[p] - rowdot)).astype(jnp.bfloat16)
                    span = pl.ds(pl.multiple_of(i * rows, 128), piece * rows)
                    dvt += dot(gt[:, span], probs.astype(jnp.bfloat16), NN)
                    dkt += dot(qt[:, span], dscores, NN)
                    kept[pl.ds(pl.multiple_of(i * rows, 128), piece * rows), 0:length] = dscores
            part[1, 0:length, lanes(k, HD)] = dvt.T.astype(jnp.bfloat16)
            part[0, 0:length, lanes(k, HD)] = (dkt.T * SCALE).astype(jnp.bfloat16)
            for dst in range(m):
                send_part(0, k, m, dst).start()
                send_part(1, k, m, dst).start()

        @pl.loop(0, KVH)
        def _(k):
            first = k * GROUP
            dscores = kept[pl.ds(pl.multiple_of(first * rows, 128), GROUP * rows), 0:length]
            grad = dot(dscores, kv[0, 0:length, lanes(k, HD)], NN) * SCALE
            for h in range(GROUP):
                dq[:, lanes(first + h, HD)] = grad[h * rows:(h + 1) * rows].astype(jnp.bfloat16)

        mine = pl.ds(m * rows, rows)
        if m < n - 1:
            for k in range(KVH):
                for which in range(2):
                    total = part[which, mine, lanes(k, HD)].astype(jnp.float32)
                    for src in range(m + 1, n):
                        send_part(which, k, src, src).wait_recv()
                        total += got[which, pl.ds(src * rows, rows), lanes(k, HD)].astype(
                            jnp.float32
                        )
                    (dk, dv)[which][:, lanes(k, HD)] = total.astype(jnp.bfloat16)
        else:
            dk[...] = part[0, mine, :]
            dv[...] = part[1, mine, :]
        for k in range(KVH):
            for which in range(2):
                for dst in range(m + 1, n):
                    send_kv(which, k, m, dst).wait_send()
                for dst in range(m):
                    send_part(which, k, m, dst).wait_send()

    for m in range(n):
        pl.when(me == m)(functools.partial(on_device, m))


def write_out(*refs):
    sources, targets, sem = refs[:4], refs[4:8], refs[8]
    copies = []
    for index in range(4):
        pieces = 4 if index < 2 else 1
        step = sources[index].shape[0] // pieces
        for piece in range(pieces):
            part = pl.ds(piece * step, step)
            copies.append(
                pltpu.make_async_copy(
                    sources[index].at[part], targets[index].at[part], sem.at[index, piece]
                )
            )
    for copy in copies:
        copy.start()
    for copy in copies:
        copy.wait()


def shards(n, queries, keys, values, lengths, out_grad):
    rows = queries.shape[0]
    segs = lengths.shape[1]
    total = n * rows
    bf16 = jnp.bfloat16
    dma = pltpu.SemaphoreType.DMA
    wide = jax.ShapeDtypeStruct(queries.shape, bf16)
    thin = jax.ShapeDtypeStruct(keys.shape, bf16)
    anywhere = pl.BlockSpec(memory_space=pl.ANY)
    held = pl.pallas_call(
        functools.partial(kernel, n, rows, segs),
        out_shape=tuple(pltpu.VMEM(x.shape, bf16) for x in (wide, wide, thin, thin)),
        in_specs=[pl.BlockSpec(memory_space=pltpu.HBM)] * 5,
        out_specs=(pl.BlockSpec(memory_space=pltpu.VMEM),) * 4,
        scratch_shapes=[
            pltpu.SMEM(lengths.shape, jnp.int32),
            pltpu.VMEM((rows, H * HD), bf16),
            pltpu.VMEM((rows, H * HD), bf16),
            pltpu.VMEM((HD, H * rows), bf16),
            pltpu.VMEM((HD, H * rows), bf16),
            pltpu.VMEM((H * rows, total), bf16),
            pltpu.VMEM((rows, total), jnp.float32),
            pltpu.VMEM((2, total, KVH * HD), bf16),
            pltpu.VMEM((2, total, KVH * HD), bf16),
            pltpu.VMEM((2, total, KVH * HD), bf16),
            dma(()),
            dma((2, KVH)),
            dma((2,)),
            dma((2, KVH, n)),
            dma((2, KVH, n)),
            dma((2, KVH, n)),
            dma((2, KVH, n)),
        ],
        compiler_params=pltpu.CompilerParams(
            collective_id=0, has_side_effects=True, vmem_limit_bytes=48 * 1024 * 1024
        ),
    )(*(
        pltpu.with_memory_space_constraint(x, pltpu.HBM)
        for x in (lengths, queries, keys, values, out_grad)
    ))
    return pl.pallas_call(
        write_out,
        out_shape=(wide, wide, thin, thin),
        in_specs=[anywhere] * 4,
        out_specs=(pl.BlockSpec(memory_space=pltpu.HBM),) * 4,
        scratch_shapes=[dma((4, 4))],
        compiler_params=pltpu.CompilerParams(vmem_limit_bytes=1024 * 1024),
    )(*(pltpu.with_memory_space_constraint(x, pltpu.VMEM) for x in held))


def solution(mesh):
    rows = P(("dp", "seq"), None)
    return jax.shard_map(
        functools.partial(shards, mesh.shape["seq"]),
        mesh=mesh,
        in_specs=(rows, rows, rows, P("dp", None), rows),
        out_specs=(rows,) * 4,
        check_vma=False,
    )
```
